32 devices in a mesh: tx: 8 (over z, core), ty: 2 (over y), mode: 2 (over x).
Axes of the slice: x: 2, y: 2, z: 4, core: 2. Of those that a mesh axis runs over, the one named last changes fastest.
Arguments:
- obj: float32 [2, 2048, 2048], P(None, 'tx', 'ty'), may hold values from -4 to 4
- probe: float32 [4, 2, 256, 256], P('mode'), may hold values from -4 to 4
- intensity: float32 [8, 2, 2, 256, 256], P('tx', 'ty'), may hold values from 0 to 2
- offsets: int32 [8, 2, 2, 2], P('tx', 'ty'), may hold values from 0 to 1023, as said below
- counts: int32 [8, 2], P('tx', 'ty'), may hold values from 1 to 2, as said below
- patch_filters: float32 [16, 4], replicated, may hold values from -2 to 2
Outputs:
- new_obj: float32 [2, 2048, 2048], P(None, 'tx', 'ty')
The draws below stay inside these ranges and needn't reach their ends.
Inputs may be any that keep to these rules, and one draw needn't show every extreme that they name: Row offsets are below 256, column offsets below 1024; a pattern may reach into the tiles below and to the right. Slots from counts[a,b] on are empty.
All inputs are finite; a program needn't handle non-finite values.
Results may differ from the reference program's by a relative error of at most 0.00012.
Values sent between devices are 32-bit elements; how exact they have to be, the bound alone decides.
A program may use at most 128 MiB of HBM per device.

```python
import math
import jax
import jax.numpy as jnp
from jax import lax

P_SIZE = 256
MODES = 4
FILT = 16
TH = 256
TW = 1024
CAP = 2
NH = 2048
NW = 2048
N_TX = 8
N_TY = 2


def draw_offsets(key, part):
    key_rows, key_cols, key_pick, key_other = jax.random.split(jax.random.fold_in(key, 11), 4)
    tiles = N_TX * N_TY
    rows = jax.random.randint(key_rows, (tiles, CAP), 0, TH)
    cols = jax.random.randint(key_cols, (tiles, CAP), 0, TW)
    rows = rows.at[jax.random.randint(key_pick, (), 0, tiles), 0].set(TH - 1)
    cols = cols.at[jax.random.randint(key_other, (), 0, tiles), 0].set(TW - 1)
    stacked = jnp.stack([rows, cols], axis=-1)
    return stacked.reshape(N_TX, N_TY, CAP, 2).astype(jnp.int32)


def draw_counts(key, part):
    key_counts, key_pick = jax.random.split(jax.random.fold_in(key, 23), 2)
    tiles = N_TX * N_TY
    counts = jax.random.randint(key_counts, (tiles,), CAP // 2, CAP + 1)
    counts = counts.at[jax.random.randint(key_pick, (), 0, tiles)].set(CAP)
    return counts.reshape(N_TX, N_TY).astype(jnp.int32)


def level_of(key, dims, shards, smallest, high):
    def one(position, shards_of):
        draws = jax.random.uniform(jax.random.fold_in(jax.random.fold_in(key, 6), position), (shards_of,), jnp.float32, smallest / len(shards), high / len(shards))
        return jnp.repeat(jnp.exp(draws), dims[position] // shards_of).reshape((-1,) + (1,) * (len(dims) - position - 1))

    loudness = one(*shards[0])
    for cut in shards[1:]:
        loudness = loudness * one(*cut)
    return loudness


def bell_draw(key, shape, spread, most, cuts=(), held_as=jnp.bfloat16):
    level = level_of(key, shape, cuts, -0.22, 0.18) if cuts else 1.0
    entries = jax.random.normal(key, shape, jnp.float32) * spread * level
    return jnp.minimum(jnp.maximum(entries, -most), most).astype(held_as)


def setup_inputs(seed: int = 0) -> dict:
    key_of = jax.random.split(jax.random.key(seed), 7)
    obj = bell_draw(key_of[0], (2, NH, NW), 0.5, 4.0, ((1, 8), (2, 2)), jnp.float32)
    probe = bell_draw(key_of[1], (MODES, 2, P_SIZE, P_SIZE), 0.5, 4.0, ((0, 2),), jnp.float32)
    intensity = jnp.clip(2.0 * jax.random.uniform(key_of[2], (N_TX, N_TY, CAP, P_SIZE, P_SIZE), jnp.float32) ** level_of(key_of[2], (N_TX, N_TY, CAP, P_SIZE, P_SIZE), ((0, 8), (1, 2)), -0.2, 0.2), 0.0, 2.0)
    offsets = draw_offsets(jax.random.fold_in(key_of[6], 71), 0)
    counts = draw_counts(jax.random.fold_in(key_of[6], 71), 0)
    patch_filters = bell_draw(key_of[5], (FILT, 4), 0.25, 2.0, (), jnp.float32)
    return {"obj": obj, "probe": probe, "intensity": intensity, "offsets": offsets, "counts": counts, "patch_filters": patch_filters}


highest = lax.Precision.HIGHEST
step_size = 0.25

def tables(length):
    ramp = jnp.arange(length, dtype=jnp.int32)
    product = ramp[:, None] * ramp[None, :] % length
    angle = product.astype(jnp.float32) * (2.0 * math.pi / length)
    scale = 1.0 / math.sqrt(length)
    return (jnp.cos(angle) * scale, -jnp.sin(angle) * scale)

def transform(real_part, imag_part, cos_tab, sin_tab):
    first_re = jnp.einsum('...k,kl->...l', real_part, cos_tab, precision=highest) - jnp.einsum('...k,kl->...l', imag_part, sin_tab, precision=highest)
    first_im = jnp.einsum('...k,kl->...l', real_part, sin_tab, precision=highest) + jnp.einsum('...k,kl->...l', imag_part, cos_tab, precision=highest)
    second_re = jnp.einsum('jk,...kl->...jl', cos_tab, first_re, precision=highest) - jnp.einsum('jk,...kl->...jl', sin_tab, first_im, precision=highest)
    second_im = jnp.einsum('jk,...kl->...jl', cos_tab, first_im, precision=highest) + jnp.einsum('jk,...kl->...jl', sin_tab, first_re, precision=highest)
    return (second_re, second_im)

def slot_grads(patches, probe, measured, cos_tab, sin_tab):
    probe_re = probe[None, :, 0]
    probe_im = probe[None, :, 1]
    obj_re = patches[:, None, 0]
    obj_im = patches[:, None, 1]
    exit_re = probe_re * obj_re - probe_im * obj_im
    exit_im = probe_re * obj_im + probe_im * obj_re
    wave_re, wave_im = transform(exit_re, exit_im, cos_tab, sin_tab)
    power = lax.optimization_barrier(jnp.sum(wave_re * wave_re + wave_im * wave_im, axis=1))
    resid = (power - measured)[:, None]
    back_re, back_im = transform(resid * wave_re, resid * wave_im, cos_tab, -sin_tab)
    grad_re = lax.optimization_barrier(jnp.sum(probe_re * back_re + probe_im * back_im, axis=1))
    grad_im = lax.optimization_barrier(jnp.sum(probe_re * back_im - probe_im * back_re, axis=1))
    return jnp.stack([grad_re, grad_im], axis=1)

def prior_term(window, filters, rows, cols):
    gram = jnp.dot(filters.T, filters, precision=highest)
    corners = [window[:, :rows, :cols], window[:, :rows, 1:], window[:, 1:, :cols], window[:, 1:, 1:]]
    mixed = [gram[which, 0] * corners[0] + gram[which, 1] * corners[1] + gram[which, 2] * corners[2] + gram[which, 3] * corners[3] for which in range(4)]
    total = jnp.pad(mixed[0], ((0, 0), (0, 1), (0, 1))) + jnp.pad(mixed[1], ((0, 0), (0, 1), (1, 0)))
    return total + jnp.pad(mixed[2], ((0, 0), (1, 0), (0, 1))) + jnp.pad(mixed[3], ((0, 0), (1, 0), (1, 0)))

def reference(obj, probe, intensity, offsets, counts, patch_filters):
    rows, cols = (obj.shape[1], obj.shape[2])
    padded = jnp.pad(obj, ((0, 0), (0, P_SIZE), (0, P_SIZE)))
    cos_tab, sin_tab = tables(P_SIZE)
    slots = N_TX * N_TY * CAP
    measured = intensity.reshape(slots, P_SIZE, P_SIZE)
    flat_offsets = offsets.reshape(slots, 2).astype(jnp.int32)
    ramp = jnp.arange(slots, dtype=jnp.int32)
    tile_row = ramp // (N_TY * CAP)
    tile_col = ramp // CAP % N_TY
    live = (ramp % CAP < counts.reshape(-1)[ramp // CAP]).astype(jnp.float32)
    zero = jnp.zeros((), jnp.int32)

    def add_slot(index, accum):
        row0 = (tile_row[index] * TH + flat_offsets[index, 0]).astype(jnp.int32)
        col0 = (tile_col[index] * TW + flat_offsets[index, 1]).astype(jnp.int32)
        patch = lax.dynamic_slice(padded, (zero, row0, col0), (2, P_SIZE, P_SIZE))
        grad = slot_grads(patch[None], probe, measured[index][None], cos_tab, sin_tab)[0] * live[index]
        current = lax.dynamic_slice(accum, (zero, row0, col0), (2, P_SIZE, P_SIZE))
        return lax.dynamic_update_slice(accum, current + grad, (zero, row0, col0))
    accum = lax.fori_loop(0, slots, add_slot, jnp.zeros(padded.shape, jnp.float32))
    prior = prior_term(padded[:, :rows + 1, :cols + 1], patch_filters, rows, cols)
    total = accum[:, :rows + 1, :cols + 1] + prior
    return obj - step_size * total[:, :rows, :cols]
```

```python
import functools
import math

import jax
import jax.numpy as jnp
import ml_dtypes
import numpy as np
from jax import lax
from jax.experimental import pallas as pl
from jax.experimental.pallas import tpu as pltpu
from jax.sharding import PartitionSpec as P

highest = lax.Precision.HIGHEST
step_size = 0.25


def shift(value, steps_tx, steps_ty, tx, ty):
    if steps_tx and steps_ty:
        pairs = []
        for a in range(tx):
            for b in range(ty):
                to_a, to_b = a + steps_tx, b + steps_ty
                if 0 <= to_a < tx and 0 <= to_b < ty:
                    pairs.append((a * ty + b, to_a * ty + to_b))
        return lax.ppermute(value, ("tx", "ty"), pairs)
    axis, count, steps = ("tx", tx, steps_tx) if steps_tx else ("ty", ty, steps_ty)
    pairs = [(i, i + steps) for i in range(count) if 0 <= i + steps < count]
    return lax.ppermute(value, axis, pairs)


def split(value):
    top = value.astype(np.float32).astype(ml_dtypes.bfloat16)
    rest = (value - top.astype(np.float64)).astype(ml_dtypes.bfloat16)
    return top, rest


def tables(length):
    ramp = np.arange(length)
    angle = (ramp[:, None] * ramp[None, :] % length) * (2.0 * math.pi / length)
    c = np.cos(angle) / math.sqrt(length)
    s = -np.sin(angle) / math.sqrt(length)
    plain = np.block([[c, s], [-s, c]])
    conj = np.block([[c, -s], [s, c]])
    out = []
    for table in (plain, conj):
        top, rest = split(table)
        out.append(np.concatenate([top, top, rest], axis=0))
        out.append(np.concatenate([top, top, rest], axis=1))
    return out


def halves(value):
    top = value.astype(jnp.bfloat16)
    rest = (value - top.astype(jnp.float32)).astype(jnp.bfloat16)
    return top, rest


def dot_right(value, table):
    top, rest = halves(value)
    return jnp.dot(jnp.concatenate([top, rest, top], axis=1), table, preferred_element_type=jnp.float32)


def dot_left(table, value):
    top, rest = halves(value)
    return jnp.dot(table, jnp.concatenate([top, rest, top], axis=0), preferred_element_type=jnp.float32)


def slot_kernel(place_ref, patch_ref, probe_ref, measured_ref, pr_ref, pl_ref, cr_ref, cl_ref, grad_ref, wave_ref, rolled_ref, power_ref):
    modes, width = probe_ref.shape[0], probe_ref.shape[-1]
    row, col, live = place_ref[0], place_ref[1], place_ref[2]
    power_ref[...] = jnp.zeros_like(power_ref)
    grad_ref[...] = jnp.zeros_like(grad_ref)

    def stacked(flat):
        return jnp.concatenate([flat[:, :width], flat[:, width:]], axis=0)

    def forward(mode, _):
        for part in range(2):
            turned = pltpu.roll(probe_ref[mode, part], row, 0)
            rolled_ref[mode, part] = pltpu.roll(turned, col, 1)
        probe_re, probe_im = rolled_ref[mode, 0], rolled_ref[mode, 1]
        obj_re, obj_im = patch_ref[0], patch_ref[1]
        exit_wave = jnp.concatenate(
            [probe_re * obj_re - probe_im * obj_im, probe_re * obj_im + probe_im * obj_re], axis=1
        )
        wave = dot_left(cl_ref[...], stacked(dot_right(exit_wave, pr_ref[...])))
        wave_ref[mode] = wave
        power_ref[...] += wave[:width] * wave[:width] + wave[width:] * wave[width:]
        return 0

    def backward(mode, _):
        resid = power_ref[...]
        bent = jnp.concatenate([resid * wave_ref[mode, :width], resid * wave_ref[mode, width:]], axis=1)
        back = dot_left(pl_ref[...], stacked(dot_right(bent, cr_ref[...])))
        probe_re, probe_im = rolled_ref[mode, 0], rolled_ref[mode, 1]
        grad_ref[0] += probe_re * back[:width] + probe_im * back[width:]
        grad_ref[1] += probe_re * back[width:] - probe_im * back[:width]
        return 0

    lax.fori_loop(0, modes, forward, 0)
    power_ref[...] = jnp.where(live > 0, power_ref[...] - measured_ref[...], 0.0)
    lax.fori_loop(0, modes, backward, 0)


def slot_grad(place, patch, probe, measured):
    modes, width = probe.shape[0], probe.shape[-1]
    vmem = pl.BlockSpec(memory_space=pltpu.VMEM)
    work = 16 * modes * width**3 * 2 * 3
    return pl.pallas_call(
        slot_kernel,
        out_shape=jax.ShapeDtypeStruct(patch.shape, jnp.float32),
        in_specs=[pl.BlockSpec(memory_space=pltpu.SMEM)] + [vmem] * 7,
        out_specs=vmem,
        scratch_shapes=[
            pltpu.VMEM((modes, 2 * width, width), jnp.float32),
            pltpu.VMEM(probe.shape, jnp.float32),
            pltpu.VMEM((width, width), jnp.float32),
        ],
        compiler_params=pltpu.CompilerParams(vmem_limit_bytes=40 * 2**20),
        cost_estimate=pl.CostEstimate(flops=work, bytes_accessed=8 * 2**20, transcendentals=0),
        name="slot_grad",
    )(place, patch, probe, measured, *[jnp.asarray(t) for t in tables(width)])


def final_kernel(place_ref, base_ref, own_ref, other_ref, up_ref, up_other_ref, spill_ref, out_ref):
    width = own_ref.shape[-1]
    block = pl.program_id(0)
    shape = (width, width)
    rows = lax.broadcasted_iota(jnp.int32, shape, 0)
    cols = lax.broadcasted_iota(jnp.int32, shape, 1) + block * width
    masks = []
    for which in range(4):
        row, col = place_ref[2 * which], place_ref[2 * which + 1]
        inside = (cols >= col) & (cols < col + width)
        masks.append(inside & ((rows >= row) if which < 2 else (rows < row)))
    first = block == 0
    for part in range(2):
        total = jnp.where(first, spill_ref[part], 0.0)
        for mask, ref in zip(masks, (own_ref, other_ref, up_ref, up_other_ref)):
            total += jnp.where(mask, ref[part], 0.0)
        out_ref[part] = base_ref[part] - step_size * total


def final(place, base, own, other, up, up_other, spill):
    width = own.shape[-1]
    blocks = base.shape[2] // width
    whole = pl.BlockSpec((2, width, width), lambda k: (0, 0, 0))
    strip = pl.BlockSpec((2, width, width), lambda k: (0, 0, k))
    return pl.pallas_call(
        final_kernel,
        grid=(blocks,),
        out_shape=jax.ShapeDtypeStruct(base.shape, jnp.float32),
        in_specs=[pl.BlockSpec(memory_space=pltpu.SMEM), strip] + [whole] * 5,
        out_specs=strip,
        compiler_params=pltpu.CompilerParams(vmem_limit_bytes=40 * 2**20),
        name="final",
    )(place, base, own, other, up, up_other, spill)


def prior_base(obj, gram, top, bottom, left, right, first_row, first_col):
    tall = jnp.concatenate([top, obj, bottom], axis=1)
    window = jnp.concatenate([left, tall, right], axis=2)
    rows, cols = obj.shape[1], obj.shape[2]
    above, here, below = window[:, :rows], window[:, 1 : rows + 1], window[:, 2:]
    inner_row = jnp.logical_not(first_row & (jnp.arange(rows) == 0)).astype(jnp.float32)[None, :, None]
    inner_col = jnp.logical_not(first_col & (jnp.arange(cols) == 0)).astype(jnp.float32)[None, None, :]
    g = gram
    a = here[:, :, 1:-1]
    b = below[:, :, 1:-1]
    u = above[:, :, 1:-1]
    middle = g[0, 0] * a + g[0, 2] * b + inner_row * (g[2, 0] * u + g[2, 2] * a)
    middle += inner_col * (g[1, 1] * a + g[1, 3] * b + inner_row * (g[3, 1] * u + g[3, 3] * a))
    a, b, u = here[:, :, 2:], below[:, :, 2:], above[:, :, 2:]
    middle += g[0, 1] * a + g[0, 3] * b + inner_row * (g[2, 1] * u + g[2, 3] * a)
    a, b, u = here[:, :, :-2], below[:, :, :-2], above[:, :, :-2]
    middle += inner_col * (g[1, 0] * a + g[1, 2] * b + inner_row * (g[3, 0] * u + g[3, 2] * a))
    return obj - step_size * middle


def fold(tile, right, col):
    width = right.shape[2]
    ramp = jnp.arange(width, dtype=jnp.int32)[None, None, :]
    start = tile.shape[2]
    total = jnp.where(start + ramp < col + width, right, 0.0)
    for k in range(tile.shape[2] // width):
        place = k * width + ramp
        total = jnp.where((place >= col) & (place < col + width), tile[:, :, k * width : (k + 1) * width], total)
    return total


def local(tx, ty, obj, probe, intensity, offsets, counts, patch_filters):
    rows, cols = obj.shape[1], obj.shape[2]
    width = intensity.shape[-1]
    move = functools.partial(shift, tx=tx, ty=ty)
    here_tx, here_ty, mode = lax.axis_index("tx"), lax.axis_index("ty"), lax.axis_index("mode")

    tile_offsets = offsets[0, 0]
    up_offsets = move(tile_offsets, 1, 0)
    right = move(obj[:, :, :width], 0, -1)

    local_modes = probe.shape[0]
    half = local_modes // 2
    odd = lax.rem(here_tx, 2)
    mine = lax.dynamic_slice_in_dim(probe, odd * half, half, 0)
    fetched = lax.ppermute(mine, "mode", [(0, 1), (1, 0)])
    traded = lax.ppermute(fetched, "tx", [(i, i ^ 1) for i in range(tx)])
    chosen_probe = jnp.concatenate([probe, fetched, traded], axis=0)

    gram = jnp.dot(patch_filters.T, patch_filters, precision=highest)
    top = move(obj[:, rows - 1 :, :], 1, 0)
    bottom = move(obj[:, :1, :], -1, 0)
    edge_last = jnp.concatenate([top[:, :, -1:], obj[:, :, -1:], bottom[:, :, -1:]], axis=1)
    edge_first = jnp.concatenate([top[:, :, :1], obj[:, :, :1], bottom[:, :, :1]], axis=1)
    halo_left = move(edge_last, 0, 1)
    halo_right = move(edge_first, 0, -1)
    base = prior_base(obj, gram, top, bottom, halo_left, halo_right, here_tx == 0, here_ty == 0)

    my_place = lax.dynamic_index_in_dim(tile_offsets, mode, 0, False)
    my_up = lax.dynamic_index_in_dim(up_offsets, mode, 0, False)
    measured = lax.dynamic_index_in_dim(intensity[0, 0], mode, 0, False)
    below = move(fold(obj, right, my_up[1]), -1, 0)
    ramp = jnp.arange(width, dtype=jnp.int32)
    patch = jnp.where(ramp[None, :, None] >= my_place[0], fold(obj, right, my_place[1]), below)
    live = (mode < counts[0, 0]).astype(jnp.int32)
    place = jnp.stack([my_place[0] % width, my_place[1] % width, live])
    grad = slot_grad(place, patch, chosen_probe, measured)

    other = lax.ppermute(grad, "mode", [(0, 1), (1, 0)])
    up = move(grad, 1, 0)
    up_other = move(other, 1, 0)
    your_place = lax.dynamic_index_in_dim(tile_offsets, 1 - mode, 0, False)
    your_up = lax.dynamic_index_in_dim(up_offsets, 1 - mode, 0, False)

    row_ramp, col_ramp = ramp[None, :, None], ramp[None, None, :]

    def spilled(value, at, own):
        seen = col_ramp + cols < at[1] + width
        return jnp.where(seen & ((row_ramp >= at[0]) if own else (row_ramp < at[0])), value, 0.0)

    leaving = spilled(grad, my_place, True) + spilled(other, your_place, True)
    leaving += spilled(up, my_up, False) + spilled(up_other, your_up, False)
    spill = move(leaving, 0, 1)
    places = jnp.concatenate([my_place, your_place, my_up, your_up])
    return final(places, base, grad, other, up, up_other, spill)


def solution(mesh):
    placed = (
        P(None, "tx", "ty"),
        P("mode", None, None, None),
        P("tx", "ty", None, None, None),
        P("tx", "ty", None, None),
        P("tx", "ty"),
        P(),
    )
    return jax.shard_map(
        functools.partial(local, mesh.shape["tx"], mesh.shape["ty"]),
        mesh=mesh,
        in_specs=placed,
        out_specs=P(None, "tx", "ty"),
        check_vma=False,
    )
```

```python
import functools
import math

import jax
import jax.numpy as jnp
import ml_dtypes
import numpy as np
from jax import lax
from jax.experimental import pallas as pl
from jax.experimental.pallas import tpu as pltpu
from jax.sharding import PartitionSpec as P

step_size = 0.25


def split(value):
    top = value.astype(np.float32).astype(ml_dtypes.bfloat16)
    rest = (value - top.astype(np.float64)).astype(ml_dtypes.bfloat16)
    return top, rest


def tables(length):
    ramp = np.arange(length)
    angle = (ramp[:, None] * ramp[None, :] % length) * (2.0 * math.pi / length)
    c = np.cos(angle) / math.sqrt(length)
    s = -np.sin(angle) / math.sqrt(length)
    plain = np.block([[c, s], [-s, c]])
    conj = np.block([[c, -s], [s, c]])
    out = []
    for table in (plain, conj):
        top, rest = split(table)
        out.append(np.concatenate([top, top, rest], axis=0))
        out.append(np.concatenate([top, top, rest], axis=1))
    return out


def halves(value):
    top = value.astype(jnp.bfloat16)
    rest = (value - top.astype(jnp.float32)).astype(jnp.bfloat16)
    return top, rest


def dot_right(value, table):
    top, rest = halves(value)
    return jnp.dot(jnp.concatenate([top, rest, top], axis=1), table, preferred_element_type=jnp.float32)


def dot_left(table, value):
    top, rest = halves(value)
    return jnp.dot(table, jnp.concatenate([top, rest, top], axis=0), preferred_element_type=jnp.float32)


MESH = pl.DeviceIdType.MESH
COPIES = 22


def step_kernel(
    tx, ty,
    offsets_ref, counts_ref, filters_ref, obj_hbm, probe_ref, intensity_hbm, pr_hbm, pl_hbm, cr_hbm, cl_hbm,
    out_ref,
    tall_ref, left_ref, right_ref, send_place, up_place, fetched_ref, traded_ref, turned_ref, fold_ref, up_fold_ref,
    below_ref, wave_ref, power_ref, measured_ref, grad_ref, other_ref, up_ref, up_other_ref, leave_ref, spill_ref,
    pr_ref, pl_ref, cr_ref, cl_ref, send_sem, recv_sem, local_sem,
):
    a, b, m = lax.axis_index("tx"), lax.axis_index("ty"), lax.axis_index("mode")
    rows, cols = obj_hbm.shape[1], obj_hbm.shape[2]
    width = power_ref.shape[-1]
    local_modes = probe_ref.shape[0]
    half = local_modes // 2
    modes = 2 * local_modes
    up = (lax.rem(a + tx - 1, tx), b, m)
    down = (lax.rem(a + 1, tx), b, m)
    left = (a, lax.rem(b + ty - 1, ty), m)
    right = (a, lax.rem(b + 1, ty), m)
    partner = (a, b, 1 - m)
    odd = lax.rem(a, 2)
    pair = (a + 1 - 2 * odd, b, m)

    def send(which, src, dst, target):
        copy = pltpu.make_async_remote_copy(
            src_ref=src, dst_ref=dst, send_sem=send_sem.at[which], recv_sem=recv_sem.at[which],
            device_id=target, device_id_type=MESH,
        )
        copy.start()
        return copy

    middle = pl.ds(8, rows)
    fetches = [
        pltpu.make_async_copy(src, dst, local_sem.at[k])
        for k, (src, dst) in enumerate((
            (obj_hbm, tall_ref.at[:, middle, :]),
            (intensity_hbm.at[0, 0, m], measured_ref),
            (pr_hbm, pr_ref), (cl_hbm, cl_ref), (cr_hbm, cr_ref), (pl_hbm, pl_ref),
        ))
    ]
    for fetch in fetches:
        fetch.start()

    row, col = offsets_ref[0, 0, m, 0], offsets_ref[0, 0, m, 1]
    your_row, your_col = offsets_ref[0, 0, 1 - m, 0], offsets_ref[0, 0, 1 - m, 1]
    for k, value in enumerate((row, col, your_row, your_col)):
        send_place[8 * k : 8 * k + 8] = jnp.full((8, width), value, jnp.int32)

    barrier = pltpu.get_barrier_semaphore()
    for target in (up, down, left, right, partner):
        pl.semaphore_signal(barrier, inc=1, device_id=target, device_id_type=MESH)
    pl.semaphore_wait(barrier, 5)

    copies = {}
    copies[0] = send(0, send_place, up_place, down)
    for part in range(2):
        copies[1 + part] = send(
            1 + part, obj_hbm.at[part, :, pl.ds(0, width)], right_ref.at[part, middle, :], left
        )
    copies[3] = send(3, probe_ref.at[pl.ds(odd * half, half)], fetched_ref, partner)
    copies[5] = send(5, obj_hbm.at[:, pl.ds(rows - 8, 8), :], tall_ref.at[:, pl.ds(0, 8), :], down)
    copies[6] = send(6, obj_hbm.at[:, pl.ds(0, 8), :], tall_ref.at[:, pl.ds(rows + 8, 8), :], up)
    copies[7] = send(7, obj_hbm.at[:, :, pl.ds(cols - 128, 128)], left_ref.at[:, middle, :], right)

    row_turn, col_turn = lax.rem(row, width), lax.rem(col, width)

    def turn(source, first, count):
        def one(mode, _):
            for part in range(2):
                turned = pltpu.roll(source[mode, part], row_turn, 0)
                turned_ref[first + mode, part] = pltpu.roll(turned, col_turn, 1)
            return 0

        lax.fori_loop(0, count, one, 0)

    shape = (width, width)
    row_ramp = lax.broadcasted_iota(jnp.int32, shape, 0)
    col_ramp = lax.broadcasted_iota(jnp.int32, shape, 1)

    def fold(part, at):
        total = jnp.where((col_ramp + cols < at + width) & (b < ty - 1), right_ref[part, middle, :], 0.0)
        for k in range(cols // width):
            place = col_ramp + k * width
            seen = (place >= at) & (place < at + width)
            total = jnp.where(seen, tall_ref[part, middle, k * width : (k + 1) * width], total)
        return total

    turn(probe_ref, 0, local_modes)
    fetches[0].wait()
    copies[0].wait_recv()
    copies[5].wait_recv()
    copies[6].wait_recv()
    top, bottom = pl.ds(0, 8), pl.ds(rows + 8, 8)
    copies[8] = send(8, tall_ref.at[:, top, pl.ds(cols - 128, 128)], left_ref.at[:, top, :], right)
    copies[9] = send(9, tall_ref.at[:, bottom, pl.ds(cols - 128, 128)], left_ref.at[:, bottom, :], right)
    up_row, up_col = up_place[0:1], up_place[8:9]
    up_your_row, up_your_col = up_place[16:17], up_place[24:25]
    for part in range(2):
        copies[1 + part].wait_recv()
        up_fold_ref[part] = fold(part, up_col)
        copies[12 + part] = send(12 + part, up_fold_ref.at[part], below_ref.at[part], up)
        fold_ref[part] = fold(part, col)
        if part == 0:
            copies[3].wait_recv()
            copies[4] = send(4, fetched_ref, traded_ref, pair)
            turn(fetched_ref, local_modes, half)
    copies[10] = send(10, tall_ref.at[:, top, pl.ds(0, 128)], right_ref.at[:, top, pl.ds(0, 128)], left)
    copies[11] = send(11, tall_ref.at[:, bottom, pl.ds(0, 128)], right_ref.at[:, bottom, pl.ds(0, 128)], left)
    copies[4].wait_recv()
    turn(traded_ref, local_modes + half, half)
    for fetch in fetches[1:]:
        fetch.wait()
    for part in range(2):
        copies[12 + part].wait_recv()
        below = jnp.where(a < tx - 1, below_ref[part], 0.0)
        fold_ref[part] = jnp.where(row_ramp >= row, fold_ref[part], below)

    power_ref[...] = jnp.zeros_like(power_ref)
    grad_ref[...] = jnp.zeros_like(grad_ref)

    def stacked(flat):
        return jnp.concatenate([flat[:, :width], flat[:, width:]], axis=0)

    def forward(mode, _):
        probe_re, probe_im = turned_ref[mode, 0], turned_ref[mode, 1]
        obj_re, obj_im = fold_ref[0], fold_ref[1]
        exit_wave = jnp.concatenate(
            [probe_re * obj_re - probe_im * obj_im, probe_re * obj_im + probe_im * obj_re], axis=1
        )
        wave = dot_left(cl_ref[...], stacked(dot_right(exit_wave, pr_ref[...])))
        wave_ref[mode] = wave
        power_ref[...] += wave[:width] * wave[:width] + wave[width:] * wave[width:]
        return 0

    def backward(mode, _):
        resid = power_ref[...]
        bent = jnp.concatenate([resid * wave_ref[mode, :width], resid * wave_ref[mode, width:]], axis=1)
        back = dot_left(pl_ref[...], stacked(dot_right(bent, cr_ref[...])))
        probe_re, probe_im = turned_ref[mode, 0], turned_ref[mode, 1]
        grad_ref[0] += probe_re * back[:width] + probe_im * back[width:]
        grad_ref[1] += probe_re * back[width:] - probe_im * back[:width]
        return 0

    lax.fori_loop(0, modes, forward, 0)
    power_ref[...] = jnp.where(m < counts_ref[0, 0], power_ref[...] - measured_ref[...], 0.0)
    lax.fori_loop(0, modes, backward, 0)

    for part in range(2):
        copies[14 + part] = send(14 + part, grad_ref.at[part], other_ref.at[part], partner)
        copies[16 + part] = send(16 + part, grad_ref.at[part], up_ref.at[part], down)

    gram = {}
    for i in range(4):
        for j in range(i, 4):
            total = filters_ref[0, i] * filters_ref[0, j]
            for f in range(1, filters_ref.shape[0]):
                total += filters_ref[f, i] * filters_ref[f, j]
            gram[i, j] = gram[j, i] = total
    for which in (7, 8, 9, 10, 11):
        copies[which].wait_recv()
    size = 64

    def prior(step, _):
        part = step // (rows // size)
        start = pl.multiple_of(lax.rem(step, rows // size) * size, size)

        def windows(ref, lanes):
            block = ref[part, pl.ds(start, size + 16), lanes]
            at = lax.broadcasted_iota(jnp.int32, (size, block.shape[1]), 0) + start
            low = jnp.where((at == rows - 1) & (a == tx - 1), 0.0, block[9 : size + 9])
            return block[7 : size + 7], block[8 : size + 8], low, jnp.logical_not((at == 0) & (a == 0))

        def side(sets, one, two, three, four):
            high, here, low, inner = sets
            return gram[one] * here + gram[two] * low + jnp.where(inner, gram[three] * high + gram[four] * here, 0.0)

        mid = windows(tall_ref, slice(None))
        lft = windows(left_ref, slice(None))
        rgt = windows(right_ref, slice(0, 128))
        inner_col = jnp.logical_not(
            (lax.broadcasted_iota(jnp.int32, (size, cols), 1) == 0) & (b == 0)
        )
        total = side(mid, (0, 0), (0, 2), (2, 0), (2, 2))
        ahead = side(mid, (0, 1), (0, 3), (2, 1), (2, 3))
        ahead_right = jnp.where(b < ty - 1, side(rgt, (0, 1), (0, 3), (2, 1), (2, 3)), 0.0)
        ahead = pltpu.roll(jnp.concatenate([ahead, ahead_right], axis=1), cols + 127, 1)[:, :cols]
        back = side(mid, (1, 0), (1, 2), (3, 0), (3, 2))
        back_left = side(lft, (1, 0), (1, 2), (3, 0), (3, 2))
        back = pltpu.roll(jnp.concatenate([back_left, back], axis=1), 1, 1)[:, 128:]
        back += side(mid, (1, 1), (1, 3), (3, 1), (3, 3))
        total += ahead + jnp.where(inner_col, back, 0.0)
        out_ref[part, pl.ds(start, size), :] = mid[1] - step_size * total
        return 0

    lax.fori_loop(0, 2 * (rows // size), prior, 0)

    def settle(part, values):
        for k in range(cols // width):
            place = col_ramp + k * width
            total = None
            for value, at_row, at_col, own in values:
                mask = (place >= at_col) & (place < at_col + width)
                mask &= (row_ramp >= at_row) if own else ((row_ramp < at_row) & (a > 0))
                piece = jnp.where(mask, value, 0.0)
                total = piece if total is None else total + piece
            here = slice(k * width, (k + 1) * width)
            out_ref[part, :, here] = out_ref[part, :, here] - step_size * total

    def spilled(value, at_row, at_col, own):
        mask = col_ramp + cols < at_col + width
        mask &= (row_ramp >= at_row) if own else ((row_ramp < at_row) & (a > 0))
        return jnp.where(mask, value, 0.0)

    for part in range(2):
        copies[14 + part].wait_recv()
        copies[18 + part] = send(18 + part, other_ref.at[part], up_other_ref.at[part], down)
        copies[16 + part].wait_recv()
        pieces = [
            (grad_ref[part], row, col, True),
            (other_ref[part], your_row, your_col, True),
            (up_ref[part], up_row, up_col, False),
        ]
        leave_ref[part] = spilled(*pieces[0]) + spilled(*pieces[1]) + spilled(*pieces[2])
        settle(part, pieces)
    for part in range(2):
        copies[18 + part].wait_recv()
        piece = (up_other_ref[part], up_your_row, up_your_col, False)
        leave_ref[part] = leave_ref[part] + spilled(*piece)
        copies[20 + part] = send(20 + part, leave_ref.at[part], spill_ref.at[part], right)
    for part in range(2):
        settle(part, [(up_other_ref[part], up_your_row, up_your_col, False)])
    for part in range(2):
        copies[20 + part].wait_recv()
        out_ref[part, :, :width] = out_ref[part, :, :width] - step_size * jnp.where(b > 0, spill_ref[part], 0.0)
    for which in range(COPIES):
        copies[which].wait_send()


def local(tx, ty, obj, probe, intensity, offsets, counts, patch_filters):
    rows, cols = obj.shape[1], obj.shape[2]
    width = intensity.shape[-1]
    local_modes = probe.shape[0]
    half = local_modes // 2
    modes = 2 * local_modes
    f32 = jnp.float32
    plane = (2, width, width)
    vmem = pl.BlockSpec(memory_space=pltpu.VMEM)
    smem = pl.BlockSpec(memory_space=pltpu.SMEM)
    hbm = pl.BlockSpec(memory_space=pl.ANY)
    consts = [jnp.asarray(t) for t in tables(width)]
    return pl.pallas_call(
        functools.partial(step_kernel, tx, ty),
        out_shape=jax.ShapeDtypeStruct(obj.shape, f32),
        in_specs=[smem, smem, smem, hbm, vmem, hbm] + [hbm] * 4,
        out_specs=vmem,
        scratch_shapes=[
            pltpu.VMEM((2, rows + 16, cols), f32),
            pltpu.VMEM((2, rows + 16, 128), f32),
            pltpu.VMEM((2, rows + 16, width), f32),
            pltpu.VMEM((32, width), jnp.int32),
            pltpu.VMEM((32, width), jnp.int32),
            pltpu.VMEM((half, 2, width, width), f32),
            pltpu.VMEM((half, 2, width, width), f32),
            pltpu.VMEM((modes, 2, width, width), f32),
            pltpu.VMEM(plane, f32),
            pltpu.VMEM(plane, f32),
            pltpu.VMEM(plane, f32),
            pltpu.VMEM((modes, 2 * width, width), f32),
            pltpu.VMEM((width, width), f32),
            pltpu.VMEM((width, width), f32),
        ]
        + [pltpu.VMEM(plane, f32)] * 6
        + [pltpu.VMEM(t.shape, t.dtype) for t in consts]
        + [
            pltpu.SemaphoreType.DMA((COPIES,)),
            pltpu.SemaphoreType.DMA((COPIES,)),
            pltpu.SemaphoreType.DMA((6,)),
        ],
        compiler_params=pltpu.CompilerParams(
            collective_id=0, has_side_effects=True, vmem_limit_bytes=56 * 2**20
        ),
        cost_estimate=pl.CostEstimate(
            flops=16 * modes * width**3 * 6, bytes_accessed=12 * 2**20, transcendentals=0
        ),
        name="guidance_step",
    )(offsets, counts, patch_filters, obj, probe, intensity, *consts)


def solution(mesh):
    placed = (
        P(None, "tx", "ty"),
        P("mode", None, None, None),
        P("tx", "ty", None, None, None),
        P("tx", "ty", None, None),
        P("tx", "ty"),
        P(),
    )
    return jax.shard_map(
        functools.partial(local, mesh.shape["tx"], mesh.shape["ty"]),
        mesh=mesh,
        in_specs=placed,
        out_specs=P(None, "tx", "ty"),
        check_vma=False,
    )
```

```python
import functools
import math

import jax
import jax.numpy as jnp
import ml_dtypes
import numpy as np
from jax import lax
from jax.experimental import pallas as pl
from jax.experimental.pallas import tpu as pltpu
from jax.sharding import PartitionSpec as P

step_size = 0.25


def split(value):
    top = value.astype(np.float32).astype(ml_dtypes.bfloat16)
    rest = (value - top.astype(np.float64)).astype(ml_dtypes.bfloat16)
    return top, rest


def tables(length):
    ramp = np.arange(length)
    angle = (ramp[:, None] * ramp[None, :] % length) * (2.0 * math.pi / length)
    c = np.cos(angle) / math.sqrt(length)
    s = -np.sin(angle) / math.sqrt(length)
    plain = np.block([[c, s], [-s, c]])
    conj = np.block([[c, -s], [s, c]])
    out = []
    for table in (plain, conj):
        top, rest = split(table)
        out.append(np.concatenate([top, top, rest], axis=0))
        out.append(np.concatenate([top, top, rest], axis=1))
    return out


def halves(value):
    top = value.astype(jnp.bfloat16)
    rest = (value - top.astype(jnp.float32)).astype(jnp.bfloat16)
    return top, rest


def dot_right(value, table):
    top, rest = halves(value)
    return jnp.dot(jnp.concatenate([top, rest, top], axis=1), table, preferred_element_type=jnp.float32)


def dot_left(table, value):
    top, rest = halves(value)
    return jnp.dot(table, jnp.concatenate([top, rest, top], axis=0), preferred_element_type=jnp.float32)


MESH = pl.DeviceIdType.MESH
SPLITS = 4
CHUNKS = 2 * SPLITS
COPIES = 10 + 6 * CHUNKS


def step_kernel(
    tx, ty,
    offsets_ref, counts_ref, filters_ref, obj_hbm, probe_hbm, intensity_hbm, pr_hbm, pl_hbm, cr_hbm, cl_hbm,
    out_ref,
    tall_ref, probe_ref, left_ref, right_ref, send_place, up_place, fetched_ref, traded_ref, turned_ref, fold_ref, up_fold_ref,
    below_ref, wave_ref, power_ref, measured_ref, grad_ref, other_ref, up_ref, up_other_ref, leave_ref, spill_ref,
    pr_ref, pl_ref, cr_ref, cl_ref, send_sem, recv_sem, local_sem,
):
    a, b, m = lax.axis_index("tx"), lax.axis_index("ty"), lax.axis_index("mode")
    rows, cols = obj_hbm.shape[1], obj_hbm.shape[2]
    width = power_ref.shape[-1]
    local_modes = probe_ref.shape[0]
    half = local_modes // 2
    modes = 2 * local_modes
    up = (lax.rem(a + tx - 1, tx), b, m)
    down = (lax.rem(a + 1, tx), b, m)
    left = (a, lax.rem(b + ty - 1, ty), m)
    right = (a, lax.rem(b + 1, ty), m)
    partner = (a, b, 1 - m)
    odd = lax.rem(a, 2)
    pair = (a + 1 - 2 * odd, b, m)

    has_up, has_down, has_left, has_right = a > 0, a < tx - 1, b > 0, b < ty - 1
    sent, awaited = [], {}

    def when(conditions, action):
        test = None
        for condition in conditions:
            test = condition if test is None else test & condition
        if test is None:
            action()
        else:
            pl.when(test)(action)

    def send(which, src, dst, target, go=(), come=()):
        copy = pltpu.make_async_remote_copy(
            src_ref=src, dst_ref=dst, send_sem=send_sem.at[which], recv_sem=recv_sem.at[which],
            device_id=target, device_id_type=MESH,
        )
        when(go, copy.start)
        sent.append((copy, go))
        awaited[which] = (copy, come)

    def arrive(which):
        copy, come = awaited[which]
        when(come, copy.wait_recv)

    block = rows // SPLITS

    def chunk(which):
        return which // SPLITS, which % SPLITS * block

    middle = pl.ds(8, rows)
    fetches = [
        pltpu.make_async_copy(src, dst, local_sem.at[k])
        for k, (src, dst) in enumerate((
            (probe_hbm, probe_ref),
            (obj_hbm, tall_ref.at[:, middle, :]),
            (intensity_hbm.at[0, 0, m], measured_ref),
            (pr_hbm, pr_ref), (cl_hbm, cl_ref), (cr_hbm, cr_ref), (pl_hbm, pl_ref),
        ))
    ]
    for fetch in fetches:
        fetch.start()

    row, col = offsets_ref[0, 0, m, 0], offsets_ref[0, 0, m, 1]
    your_row, your_col = offsets_ref[0, 0, 1 - m, 0], offsets_ref[0, 0, 1 - m, 1]
    for k, value in enumerate((row, col, your_row, your_col)):
        send_place[8 * k : 8 * k + 8] = jnp.full((8, width), value, jnp.int32)

    barrier = pltpu.get_barrier_semaphore()
    for target in (up, down, left, right, partner):
        pl.semaphore_signal(barrier, inc=1, device_id=target, device_id_type=MESH)
    pl.semaphore_wait(barrier, 5)

    send(0, send_place, up_place, down, (has_down,), (has_up,))
    for c in range(CHUNKS):
        part, start = chunk(c)
        send(
            10 + c, obj_hbm.at[part, pl.ds(start, block), pl.ds(0, width)],
            right_ref.at[part, pl.ds(8 + start, block), :], left, (has_left,), (has_right,),
        )
    send(1, probe_hbm.at[pl.ds(odd * half, half)], fetched_ref, partner)
    top, bottom = pl.ds(0, 8), pl.ds(rows + 8, 8)
    send(3, obj_hbm.at[:, pl.ds(rows - 8, 8), :], tall_ref.at[:, top, :], down, (has_down,), (has_up,))
    send(4, obj_hbm.at[:, pl.ds(0, 8), :], tall_ref.at[:, bottom, :], up, (has_up,), (has_down,))
    send(5, obj_hbm.at[:, :, pl.ds(cols - 128, 128)], left_ref.at[:, middle, :], right, (has_right,), (has_left,))

    row_turn, col_turn = lax.rem(row, width), lax.rem(col, width)

    def turn(source, first, count):
        def one(mode, _):
            for part in range(2):
                turned = pltpu.roll(source[mode, part], row_turn, 0)
                turned_ref[first + mode, part] = pltpu.roll(turned, col_turn, 1)
            return 0

        lax.fori_loop(0, count, one, 0)

    block_shape = (block, width)
    col_ramp = lax.broadcasted_iota(jnp.int32, block_shape, 1)

    def row_ramp(start):
        return lax.broadcasted_iota(jnp.int32, block_shape, 0) + start

    def fold(part, start, at):
        lines = slice(8 + start, 8 + start + block)
        total = jnp.where((col_ramp + cols < at + width) & has_right, right_ref[part, lines, :], 0.0)
        for k in range(cols // width):
            place = col_ramp + k * width
            seen = (place >= at) & (place < at + width)
            total = jnp.where(seen, tall_ref[part, lines, k * width : (k + 1) * width], total)
        return total

    fetches[0].wait()
    turn(probe_ref, 0, local_modes)
    fetches[1].wait()
    arrive(0)
    arrive(3)
    arrive(4)
    low, high = pl.ds(0, 128), pl.ds(cols - 128, 128)
    send(6, tall_ref.at[:, top, high], left_ref.at[:, top, :], right, (has_right, has_up), (has_left, has_up))
    send(7, tall_ref.at[:, bottom, high], left_ref.at[:, bottom, :], right, (has_right, has_down), (has_left, has_down))
    up_row, up_col = up_place[0:1], up_place[8:9]
    up_your_row, up_your_col = up_place[16:17], up_place[24:25]
    for c in range(CHUNKS):
        part, start = chunk(c)
        lines = slice(start, start + block)
        arrive(10 + c)
        up_fold_ref[part, lines] = fold(part, start, up_col)
        send(
            10 + CHUNKS + c, up_fold_ref.at[part, pl.ds(start, block)], below_ref.at[part, pl.ds(start, block)],
            up, (has_up,), (has_down,),
        )
        fold_ref[part, lines] = fold(part, start, col)
    arrive(1)
    send(2, fetched_ref, traded_ref, pair)
    send(8, tall_ref.at[:, top, low], right_ref.at[:, top, low], left, (has_left, has_up), (has_right, has_up))
    send(9, tall_ref.at[:, bottom, low], right_ref.at[:, bottom, low], left, (has_left, has_down), (has_right, has_down))
    turn(fetched_ref, local_modes, half)
    arrive(2)
    turn(traded_ref, local_modes + half, half)
    for fetch in fetches[2:]:
        fetch.wait()
    for c in range(CHUNKS):
        part, start = chunk(c)
        lines = slice(start, start + block)
        arrive(10 + CHUNKS + c)
        below = jnp.where(has_down, below_ref[part, lines], 0.0)
        fold_ref[part, lines] = jnp.where(row_ramp(start) >= row, fold_ref[part, lines], below)

    power_ref[...] = jnp.zeros_like(power_ref)
    grad_ref[...] = jnp.zeros_like(grad_ref)

    def stacked(flat):
        return jnp.concatenate([flat[:, :width], flat[:, width:]], axis=0)

    def forward(mode, _):
        probe_re, probe_im = turned_ref[mode, 0], turned_ref[mode, 1]
        obj_re, obj_im = fold_ref[0], fold_ref[1]
        exit_wave = jnp.concatenate(
            [probe_re * obj_re - probe_im * obj_im, probe_re * obj_im + probe_im * obj_re], axis=1
        )
        wave = dot_left(cl_ref[...], stacked(dot_right(exit_wave, pr_ref[...])))
        wave_ref[mode] = wave
        power_ref[...] += wave[:width] * wave[:width] + wave[width:] * wave[width:]
        return 0

    def backward(mode, _):
        resid = power_ref[...]
        bent = jnp.concatenate([resid * wave_ref[mode, :width], resid * wave_ref[mode, width:]], axis=1)
        back = dot_left(pl_ref[...], stacked(dot_right(bent, cr_ref[...])))
        probe_re, probe_im = turned_ref[mode, 0], turned_ref[mode, 1]
        grad_ref[0] += probe_re * back[:width] + probe_im * back[width:]
        grad_ref[1] += probe_re * back[width:] - probe_im * back[:width]
        return 0

    lax.fori_loop(0, modes, forward, 0)
    power_ref[...] = jnp.where(m < counts_ref[0, 0], power_ref[...] - measured_ref[...], 0.0)
    lax.fori_loop(0, modes, backward, 0)

    other_at, up_at, up_other_at, spill_at = (10 + k * CHUNKS for k in range(2, 6))

    def piece_of(ref, which):
        part, start = chunk(which)
        return ref.at[part, pl.ds(start, block)]

    for c in range(CHUNKS):
        send(other_at + c, piece_of(grad_ref, c), piece_of(other_ref, c), partner)
        send(up_at + c, piece_of(grad_ref, c), piece_of(up_ref, c), down, (has_down,), (has_up,))

    gram = {}
    for i in range(4):
        for j in range(i, 4):
            total = filters_ref[i, 0] * filters_ref[j, 0]
            for f in range(1, filters_ref.shape[1]):
                total += filters_ref[i, f] * filters_ref[j, f]
            gram[i, j] = gram[j, i] = total
    for which in range(5, 10):
        arrive(which)
    size = block

    def prior(part, start):

        def windows(ref, lanes):
            block = ref[part, pl.ds(start, size + 16), lanes]
            at = lax.broadcasted_iota(jnp.int32, (size, block.shape[1]), 0) + start
            low = jnp.where((at == rows - 1) & jnp.logical_not(has_down), 0.0, block[9 : size + 9])
            return block[7 : size + 7], block[8 : size + 8], low, jnp.logical_not((at == 0) & (a == 0))

        def side(sets, one, two, three, four):
            high, here, low, inner = sets
            return gram[one] * here + gram[two] * low + jnp.where(inner, gram[three] * high + gram[four] * here, 0.0)

        mid = windows(tall_ref, slice(None))
        lft = windows(left_ref, slice(None))
        rgt = windows(right_ref, slice(0, 128))
        inner_col = jnp.logical_not(
            (lax.broadcasted_iota(jnp.int32, (size, cols), 1) == 0) & (b == 0)
        )
        total = side(mid, (0, 0), (0, 2), (2, 0), (2, 2))
        ahead = side(mid, (0, 1), (0, 3), (2, 1), (2, 3))
        ahead_right = jnp.where(has_right, side(rgt, (0, 1), (0, 3), (2, 1), (2, 3)), 0.0)
        ahead = pltpu.roll(jnp.concatenate([ahead, ahead_right], axis=1), cols + 127, 1)[:, :cols]
        back = side(mid, (1, 0), (1, 2), (3, 0), (3, 2))
        back_left = side(lft, (1, 0), (1, 2), (3, 0), (3, 2))
        back = pltpu.roll(jnp.concatenate([back_left, back], axis=1), 1, 1)[:, 128:]
        back += side(mid, (1, 1), (1, 3), (3, 1), (3, 3))
        total += ahead + jnp.where(inner_col, back, 0.0)
        out_ref[part, pl.ds(start, size), :] = mid[1] - step_size * total

    def settle(part, start, values):
        lines = slice(start, start + block)
        ramp = row_ramp(start)
        values = [
            (jnp.where((ramp >= at_row) if own else ((ramp < at_row) & has_up), value, 0.0), at_col)
            for value, at_row, at_col, own in values
        ]
        for k in range(cols // width):
            place = col_ramp + k * width
            total = None
            for value, at_col in values:
                piece = jnp.where((place >= at_col) & (place < at_col + width), value, 0.0)
                total = piece if total is None else total + piece
            here = slice(k * width, (k + 1) * width)
            out_ref[part, lines, here] = out_ref[part, lines, here] - step_size * total

    def spilled(start, value, at_row, at_col, own):
        ramp = row_ramp(start)
        mask = col_ramp + cols < at_col + width
        mask &= (ramp >= at_row) if own else ((ramp < at_row) & has_up)
        return jnp.where(mask, value, 0.0)

    lag = 2
    for step in range(CHUNKS + lag):
        if step < CHUNKS:
            part, start = chunk(step)
            arrive(other_at + step)
            send(
                up_other_at + step, piece_of(other_ref, step), piece_of(up_other_ref, step), down,
                (has_down,), (has_up,),
            )
        if step >= lag:
            late = step - lag
            part, start = chunk(late)
            lines = slice(start, start + block)
            arrive(up_other_at + late)
            last = (up_other_ref[part, lines], up_your_row, up_your_col, False)
            leave_ref[part, lines] = leave_ref[part, lines] + spilled(start, *last)
            send(
                spill_at + late, piece_of(leave_ref, late), piece_of(spill_ref, late), right,
                (has_right,), (has_left,),
            )
            settle(part, start, [last])
        if step < CHUNKS:
            part, start = chunk(step)
            lines = slice(start, start + block)
            arrive(up_at + step)
            pieces = [
                (grad_ref[part, lines], row, col, True),
                (other_ref[part, lines], your_row, your_col, True),
                (up_ref[part, lines], up_row, up_col, False),
            ]
            leave_ref[part, lines] = (
                spilled(start, *pieces[0]) + spilled(start, *pieces[1]) + spilled(start, *pieces[2])
            )
            prior(part, start)
            settle(part, start, pieces)
    for c in range(CHUNKS):
        part, start = chunk(c)
        lines = slice(start, start + block)
        arrive(spill_at + c)
        spill = jnp.where(has_left, spill_ref[part, lines], 0.0)
        out_ref[part, lines, :width] = out_ref[part, lines, :width] - step_size * spill
    for copy, go in sent:
        when(go, copy.wait_send)


def local(tx, ty, obj, probe, intensity, offsets, counts, patch_filters):
    rows, cols = obj.shape[1], obj.shape[2]
    width = intensity.shape[-1]
    local_modes = probe.shape[0]
    half = local_modes // 2
    modes = 2 * local_modes
    f32 = jnp.float32
    plane = (2, width, width)
    vmem = pl.BlockSpec(memory_space=pltpu.VMEM)
    smem = pl.BlockSpec(memory_space=pltpu.SMEM)
    hbm = pl.BlockSpec(memory_space=pltpu.HBM)
    consts = [jnp.asarray(t) for t in tables(width)]
    return pl.pallas_call(
        functools.partial(step_kernel, tx, ty),
        out_shape=jax.ShapeDtypeStruct(obj.shape, f32),
        in_specs=[smem, smem, smem, hbm, hbm, hbm] + [hbm] * 4,
        out_specs=vmem,
        scratch_shapes=[
            pltpu.VMEM((2, rows + 16, cols), f32),
            pltpu.VMEM(probe.shape, f32),
            pltpu.VMEM((2, rows + 16, 128), f32),
            pltpu.VMEM((2, rows + 16, width), f32),
            pltpu.VMEM((32, width), jnp.int32),
            pltpu.VMEM((32, width), jnp.int32),
            pltpu.VMEM((half, 2, width, width), f32),
            pltpu.VMEM((half, 2, width, width), f32),
            pltpu.VMEM((modes, 2, width, width), f32),
            pltpu.VMEM(plane, f32),
            pltpu.VMEM(plane, f32),
            pltpu.VMEM(plane, f32),
            pltpu.VMEM((modes, 2 * width, width), f32),
            pltpu.VMEM((width, width), f32),
            pltpu.VMEM((width, width), f32),
        ]
        + [pltpu.VMEM(plane, f32)] * 6
        + [pltpu.VMEM(t.shape, t.dtype) for t in consts]
        + [
            pltpu.SemaphoreType.DMA((COPIES,)),
            pltpu.SemaphoreType.DMA((COPIES,)),
            pltpu.SemaphoreType.DMA((7,)),
        ],
        compiler_params=pltpu.CompilerParams(
            collective_id=0, has_side_effects=True, vmem_limit_bytes=40 * 2**20
        ),
        cost_estimate=pl.CostEstimate(
            flops=16 * modes * width**3 * 6, bytes_accessed=12 * 2**20, transcendentals=0
        ),
        name="guidance_step",
    )(offsets, counts, patch_filters.T, obj, probe, intensity, *consts)


def solution(mesh):
    placed = (
        P(None, "tx", "ty"),
        P("mode", None, None, None),
        P("tx", "ty", None, None, None),
        P("tx", "ty", None, None),
        P("tx", "ty"),
        P(),
    )
    return jax.shard_map(
        functools.partial(local, mesh.shape["tx"], mesh.shape["ty"]),
        mesh=mesh,
        in_specs=placed,
        out_specs=P(None, "tx", "ty"),
        check_vma=False,
    )
```

```python
import functools
import math

import jax
import jax.numpy as jnp
import ml_dtypes
import numpy as np
from jax import lax
from jax.experimental import pallas as pl
from jax.experimental.pallas import tpu as pltpu
from jax.sharding import PartitionSpec as P

step_size = 0.25


def split(value):
    top = value.astype(np.float32).astype(ml_dtypes.bfloat16)
    rest = (value - top.astype(np.float64)).astype(ml_dtypes.bfloat16)
    return top, rest


def tables(length):
    ramp = np.arange(length)
    angle = (ramp[:, None] * ramp[None, :] % length) * (2.0 * math.pi / length)
    c = np.cos(angle) / math.sqrt(length)
    s = -np.sin(angle) / math.sqrt(length)
    plain = np.block([[c, s], [-s, c]])
    conj = np.block([[c, -s], [s, c]])
    out = []
    for table in (plain, conj):
        top, rest = split(table)
        out.append(np.concatenate([top, top, rest], axis=0))
        out.append(np.concatenate([top, top, rest], axis=1))
    return out


def halves(value):
    top = value.astype(jnp.bfloat16)
    rest = (value - top.astype(jnp.float32)).astype(jnp.bfloat16)
    return top, rest


def dot_right(value, table):
    top, rest = halves(value)
    return jnp.dot(jnp.concatenate([top, rest, top], axis=1), table, preferred_element_type=jnp.float32)


def dot_left(table, value):
    top, rest = halves(value)
    return jnp.dot(table, jnp.concatenate([top, rest, top], axis=0), preferred_element_type=jnp.float32)


MESH = pl.DeviceIdType.MESH
SPLITS = 4
CHUNKS = 2 * SPLITS
COPIES = 10 + 6 * CHUNKS


def step_kernel(
    tx, ty,
    offsets_ref, counts_ref, filters_ref, obj_hbm, probe_hbm, intensity_hbm, pr_hbm, pl_hbm, cr_hbm, cl_hbm,
    out_ref,
    tall_ref, probe_ref, left_ref, right_ref, send_place, up_place, fetched_ref, traded_ref, turned_ref, fold_ref, up_fold_ref,
    below_ref, wave_ref, power_ref, measured_ref, grad_ref, other_ref, up_ref, up_other_ref, leave_ref, spill_ref,
    pr_ref, pl_ref, cr_ref, cl_ref, send_sem, recv_sem, local_sem,
):
    a, b, m = lax.axis_index("tx"), lax.axis_index("ty"), lax.axis_index("mode")
    rows, cols = obj_hbm.shape[1], obj_hbm.shape[2]
    width = power_ref.shape[-1]
    local_modes = probe_ref.shape[0]
    half = local_modes // 2
    modes = 2 * local_modes
    up = (lax.rem(a + tx - 1, tx), b, m)
    down = (lax.rem(a + 1, tx), b, m)
    left = (a, lax.rem(b + ty - 1, ty), m)
    right = (a, lax.rem(b + 1, ty), m)
    partner = (a, b, 1 - m)
    odd = lax.rem(a, 2)
    pair = (a + 1 - 2 * odd, b, m)

    has_up, has_down, has_left, has_right = a > 0, a < tx - 1, b > 0, b < ty - 1
    sent, awaited = [], {}

    def when(conditions, action):
        test = None
        for condition in conditions:
            test = condition if test is None else test & condition
        if test is None:
            action()
        else:
            pl.when(test)(action)

    def send(which, src, dst, target, go=(), come=()):
        copy = pltpu.make_async_remote_copy(
            src_ref=src, dst_ref=dst, send_sem=send_sem.at[which], recv_sem=recv_sem.at[which],
            device_id=target, device_id_type=MESH,
        )
        when(go, copy.start)
        sent.append((copy, go))
        awaited[which] = (copy, come)

    def arrive(which):
        copy, come = awaited[which]
        when(come, copy.wait_recv)

    block = rows // SPLITS

    def chunk(which):
        return which // SPLITS, which % SPLITS * block

    middle = pl.ds(8, rows)
    fetches = [
        pltpu.make_async_copy(src, dst, local_sem.at[k])
        for k, (src, dst) in enumerate((
            (probe_hbm, probe_ref),
            (obj_hbm, tall_ref.at[:, middle, :]),
            (intensity_hbm.at[0, 0, m], measured_ref),
            (pr_hbm, pr_ref), (cl_hbm, cl_ref), (cr_hbm, cr_ref), (pl_hbm, pl_ref),
        ))
    ]
    for fetch in fetches:
        fetch.start()

    row, col = offsets_ref[0, 0, m, 0], offsets_ref[0, 0, m, 1]
    your_row, your_col = offsets_ref[0, 0, 1 - m, 0], offsets_ref[0, 0, 1 - m, 1]
    for k, value in enumerate((row, col, your_row, your_col)):
        send_place[8 * k : 8 * k + 8] = jnp.full((8, width), value, jnp.int32)

    barrier = pltpu.get_barrier_semaphore()
    for target in (up, down, left, right, partner):
        pl.semaphore_signal(barrier, inc=1, device_id=target, device_id_type=MESH)
    pl.semaphore_wait(barrier, 5)

    send(0, send_place, up_place, down, (has_down,), (has_up,))
    for c in range(CHUNKS):
        part, start = chunk(c)
        send(
            10 + c, obj_hbm.at[part, pl.ds(start, block), pl.ds(0, width)],
            right_ref.at[part, pl.ds(8 + start, block), :], left, (has_left,), (has_right,),
        )
    send(1, probe_hbm.at[pl.ds(odd * half, half)], fetched_ref, partner)
    top, bottom = pl.ds(0, 8), pl.ds(rows + 8, 8)
    send(3, obj_hbm.at[:, pl.ds(rows - 8, 8), :], tall_ref.at[:, top, :], down, (has_down,), (has_up,))
    send(4, obj_hbm.at[:, pl.ds(0, 8), :], tall_ref.at[:, bottom, :], up, (has_up,), (has_down,))
    send(5, obj_hbm.at[:, :, pl.ds(cols - 128, 128)], left_ref.at[:, middle, :], right, (has_right,), (has_left,))

    row_turn, col_turn = lax.rem(row, width), lax.rem(col, width)

    def turn(source, first, count):
        def one(mode, _):
            for part in range(2):
                turned = pltpu.roll(source[mode, part], row_turn, 0)
                turned_ref[first + mode, part] = pltpu.roll(turned, col_turn, 1)
            return 0

        lax.fori_loop(0, count, one, 0)

    block_shape = (block, width)
    col_ramp = lax.broadcasted_iota(jnp.int32, block_shape, 1)

    def row_ramp(start):
        return lax.broadcasted_iota(jnp.int32, block_shape, 0) + start

    def fold(part, start, at):
        lines = slice(8 + start, 8 + start + block)
        total = jnp.where((col_ramp + cols < at + width) & has_right, right_ref[part, lines, :], 0.0)
        for k in range(cols // width):
            place = col_ramp + k * width
            seen = (place >= at) & (place < at + width)
            total = jnp.where(seen, tall_ref[part, lines, k * width : (k + 1) * width], total)
        return total

    fetches[0].wait()
    turn(probe_ref, 0, local_modes)
    fetches[1].wait()
    arrive(0)
    arrive(3)
    arrive(4)
    low, high = pl.ds(0, 128), pl.ds(cols - 128, 128)
    send(6, tall_ref.at[:, top, high], left_ref.at[:, top, :], right, (has_right, has_up), (has_left, has_up))
    send(7, tall_ref.at[:, bottom, high], left_ref.at[:, bottom, :], right, (has_right, has_down), (has_left, has_down))
    up_row, up_col = up_place[0:1], up_place[8:9]
    up_your_row, up_your_col = up_place[16:17], up_place[24:25]
    for c in range(CHUNKS):
        part, start = chunk(c)
        lines = slice(start, start + block)
        arrive(10 + c)
        up_fold_ref[part, lines] = fold(part, start, up_col)
        send(
            10 + CHUNKS + c, up_fold_ref.at[part, pl.ds(start, block)], below_ref.at[part, pl.ds(start, block)],
            up, (has_up,), (has_down,),
        )
        fold_ref[part, lines] = fold(part, start, col)
    arrive(1)
    send(2, fetched_ref, traded_ref, pair)
    send(8, tall_ref.at[:, top, low], right_ref.at[:, top, low], left, (has_left, has_up), (has_right, has_up))
    send(9, tall_ref.at[:, bottom, low], right_ref.at[:, bottom, low], left, (has_left, has_down), (has_right, has_down))
    turn(fetched_ref, local_modes, half)
    arrive(2)
    turn(traded_ref, local_modes + half, half)
    for fetch in fetches[2:]:
        fetch.wait()
    for c in range(CHUNKS):
        part, start = chunk(c)
        lines = slice(start, start + block)
        arrive(10 + CHUNKS + c)
        below = jnp.where(has_down, below_ref[part, lines], 0.0)
        fold_ref[part, lines] = jnp.where(row_ramp(start) >= row, fold_ref[part, lines], below)

    power_ref[...] = jnp.zeros_like(power_ref)
    grad_ref[...] = jnp.zeros_like(grad_ref)

    def stacked(flat):
        return jnp.concatenate([flat[:, :width], flat[:, width:]], axis=0)

    def forward(mode, _):
        probe_re, probe_im = turned_ref[mode, 0], turned_ref[mode, 1]
        obj_re, obj_im = fold_ref[0], fold_ref[1]
        exit_wave = jnp.concatenate(
            [probe_re * obj_re - probe_im * obj_im, probe_re * obj_im + probe_im * obj_re], axis=1
        )
        wave = dot_left(cl_ref[...], stacked(dot_right(exit_wave, pr_ref[...])))
        wave_ref[mode] = wave
        power_ref[...] += wave[:width] * wave[:width] + wave[width:] * wave[width:]
        return 0

    def backward(mode, _):
        resid = power_ref[...]
        bent = jnp.concatenate([resid * wave_ref[mode, :width], resid * wave_ref[mode, width:]], axis=1)
        back = dot_left(pl_ref[...], stacked(dot_right(bent, cr_ref[...])))
        probe_re, probe_im = turned_ref[mode, 0], turned_ref[mode, 1]
        grad_ref[0] += probe_re * back[:width] + probe_im * back[width:]
        grad_ref[1] += probe_re * back[width:] - probe_im * back[:width]
        return 0

    lax.fori_loop(0, modes, forward, 0)
    power_ref[...] = jnp.where(m < counts_ref[0, 0], power_ref[...] - measured_ref[...], 0.0)
    lax.fori_loop(0, modes, backward, 0)

    other_at, up_at, up_other_at, spill_at = (10 + k * CHUNKS for k in range(2, 6))

    def piece_of(ref, which):
        part, start = chunk(which)
        return ref.at[part, pl.ds(start, block)]

    for c in range(CHUNKS):
        send(other_at + c, piece_of(grad_ref, c), piece_of(other_ref, c), partner)
        send(up_at + c, piece_of(grad_ref, c), piece_of(up_ref, c), down, (has_down,), (has_up,))

    gram = {}
    for i in range(4):
        for j in range(i, 4):
            total = filters_ref[i, 0] * filters_ref[j, 0]
            for f in range(1, filters_ref.shape[1]):
                total += filters_ref[i, f] * filters_ref[j, f]
            gram[i, j] = gram[j, i] = total
    for which in range(5, 10):
        arrive(which)
    size = block

    def prior(part, start):

        def windows(ref, lanes):
            block = ref[part, pl.ds(start, size + 16), lanes]
            at = lax.broadcasted_iota(jnp.int32, (size, block.shape[1]), 0) + start
            low = jnp.where((at == rows - 1) & jnp.logical_not(has_down), 0.0, block[9 : size + 9])
            return block[7 : size + 7], block[8 : size + 8], low, jnp.logical_not((at == 0) & (a == 0))

        def side(sets, one, two, three, four):
            high, here, low, inner = sets
            return gram[one] * here + gram[two] * low + jnp.where(inner, gram[three] * high + gram[four] * here, 0.0)

        mid = windows(tall_ref, slice(None))
        lft = windows(left_ref, slice(None))
        rgt = windows(right_ref, slice(0, 128))
        inner_col = jnp.logical_not(
            (lax.broadcasted_iota(jnp.int32, (size, cols), 1) == 0) & (b == 0)
        )
        total = side(mid, (0, 0), (0, 2), (2, 0), (2, 2))
        ahead = side(mid, (0, 1), (0, 3), (2, 1), (2, 3))
        ahead_right = jnp.where(has_right, side(rgt, (0, 1), (0, 3), (2, 1), (2, 3)), 0.0)
        ahead = pltpu.roll(jnp.concatenate([ahead, ahead_right], axis=1), cols + 127, 1)[:, :cols]
        back = side(mid, (1, 0), (1, 2), (3, 0), (3, 2))
        back_left = side(lft, (1, 0), (1, 2), (3, 0), (3, 2))
        back = pltpu.roll(jnp.concatenate([back_left, back], axis=1), 1, 1)[:, 128:]
        back += side(mid, (1, 1), (1, 3), (3, 1), (3, 3))
        total += ahead + jnp.where(inner_col, back, 0.0)
        out_ref[part, pl.ds(start, size), :] = mid[1] - step_size * total

    def settle(part, start, values):
        lines = slice(start, start + block)
        ramp = row_ramp(start)
        values = [
            (jnp.where((ramp >= at_row) if own else ((ramp < at_row) & has_up), value, 0.0), at_col)
            for value, at_row, at_col, own in values
        ]
        for k in range(cols // width):
            place = col_ramp + k * width
            total = None
            for value, at_col in values:
                piece = jnp.where((place >= at_col) & (place < at_col + width), value, 0.0)
                total = piece if total is None else total + piece
            here = slice(k * width, (k + 1) * width)
            out_ref[part, lines, here] = out_ref[part, lines, here] - step_size * total

    def spilled(start, value, at_row, at_col, own):
        ramp = row_ramp(start)
        mask = col_ramp + cols < at_col + width
        mask &= (ramp >= at_row) if own else ((ramp < at_row) & has_up)
        return jnp.where(mask, value, 0.0)

    lag = 2
    for step in range(CHUNKS + lag):
        if step < CHUNKS:
            part, start = chunk(step)
            arrive(other_at + step)
            send(
                up_other_at + step, piece_of(other_ref, step), piece_of(up_other_ref, step), down,
                (has_down,), (has_up,),
            )
        if step >= lag:
            late = step - lag
            part, start = chunk(late)
            lines = slice(start, start + block)
            arrive(up_other_at + late)
            last = (up_other_ref[part, lines], up_your_row, up_your_col, False)
            leave_ref[part, lines] = leave_ref[part, lines] + spilled(start, *last)
            send(
                spill_at + late, piece_of(leave_ref, late), piece_of(spill_ref, late), right,
                (has_right,), (has_left,),
            )
            settle(part, start, [last])
        if step < CHUNKS:
            part, start = chunk(step)
            lines = slice(start, start + block)
            arrive(up_at + step)
            pieces = [
                (grad_ref[part, lines], row, col, True),
                (other_ref[part, lines], your_row, your_col, True),
                (up_ref[part, lines], up_row, up_col, False),
            ]
            leave_ref[part, lines] = (
                spilled(start, *pieces[0]) + spilled(start, *pieces[1]) + spilled(start, *pieces[2])
            )
            prior(part, start)
            settle(part, start, pieces)
    for c in range(CHUNKS):
        part, start = chunk(c)
        lines = slice(start, start + block)
        arrive(spill_at + c)
        spill = jnp.where(has_left, spill_ref[part, lines], 0.0)
        out_ref[part, lines, :width] = out_ref[part, lines, :width] - step_size * spill
    for copy, go in sent:
        when(go, copy.wait_send)


def local(tx, ty, obj, probe, intensity, offsets, counts, patch_filters):
    rows, cols = obj.shape[1], obj.shape[2]
    width = intensity.shape[-1]
    local_modes = probe.shape[0]
    half = local_modes // 2
    modes = 2 * local_modes
    f32 = jnp.float32
    plane = (2, width, width)
    vmem = pl.BlockSpec(memory_space=pltpu.VMEM)
    smem = pl.BlockSpec(memory_space=pltpu.SMEM)
    hbm = pl.BlockSpec(memory_space=pltpu.HBM)
    consts = [jnp.asarray(t) for t in tables(width)]
    return pl.pallas_call(
        functools.partial(step_kernel, tx, ty),
        out_shape=jax.ShapeDtypeStruct(obj.shape, f32),
        in_specs=[smem, smem, smem, hbm, hbm, hbm] + [hbm] * 4,
        out_specs=vmem,
        scratch_shapes=[
            pltpu.VMEM((2, rows + 16, cols), f32),
            pltpu.VMEM(probe.shape, f32),
            pltpu.VMEM((2, rows + 16, 128), f32),
            pltpu.VMEM((2, rows + 16, width), f32),
            pltpu.VMEM((32, width), jnp.int32),
            pltpu.VMEM((32, width), jnp.int32),
            pltpu.VMEM((half, 2, width, width), f32),
            pltpu.VMEM((half, 2, width, width), f32),
            pltpu.VMEM((modes, 2, width, width), f32),
            pltpu.VMEM(plane, f32),
            pltpu.VMEM(plane, f32),
            pltpu.VMEM(plane, f32),
            pltpu.VMEM((modes, 2 * width, width), f32),
            pltpu.VMEM((width, width), f32),
            pltpu.VMEM((width, width), f32),
        ]
        + [pltpu.VMEM(plane, f32)] * 6
        + [pltpu.VMEM(t.shape, t.dtype) for t in consts]
        + [
            pltpu.SemaphoreType.DMA((COPIES,)),
            pltpu.SemaphoreType.DMA((COPIES,)),
            pltpu.SemaphoreType.DMA((7,)),
        ],
        compiler_params=pltpu.CompilerParams(
            collective_id=0, has_side_effects=True, vmem_limit_bytes=57 * 2**20
        ),
        cost_estimate=pl.CostEstimate(
            flops=16 * modes * width**3 * 6, bytes_accessed=12 * 2**20, transcendentals=0
        ),
        name="guidance_step",
    )(offsets, counts, patch_filters.T, obj, probe, intensity, *consts)


def solution(mesh):
    placed = (
        P(None, "tx", "ty"),
        P("mode", None, None, None),
        P("tx", "ty", None, None, None),
        P("tx", "ty", None, None),
        P("tx", "ty"),
        P(),
    )
    return jax.shard_map(
        functools.partial(local, mesh.shape["tx"], mesh.shape["ty"]),
        mesh=mesh,
        in_specs=placed,
        out_specs=P(None, "tx", "ty"),
        check_vma=False,
    )
```
